32 devices in a mesh: replica: 8 (over y, x, core), fsdp: 4 (over z).
Axes of the slice: x: 2, y: 2, z: 4, core: 2. Of those that a mesh axis runs over, the one named last changes fastest.
Arguments:
- local_weight: bfloat16 [8, 64, 8192], P('replica', None, 'fsdp'), may hold values from -1 to 1
- anchor: float32 [64, 8192], P(None, 'fsdp'), may hold values from -0.75 to 0.75
- momentum: float32 [64, 8192], P('replica', 'fsdp'), may hold values from -0.3 to 0.3
- tokens: bfloat16 [4096, 64], P(('replica', 'fsdp')), may hold values from -6 to 6
Outputs:
- blended_weight: bfloat16 [8, 64, 8192], P('replica', None, 'fsdp')
- anchor_out: float32 [64, 8192], P(None, 'fsdp')
- momentum_out: float32 [64, 8192], P('replica', 'fsdp')
- product_out: bfloat16 [4096, 8192], P(('replica', 'fsdp'))
The draws below stay inside these ranges and needn't reach their ends.
All inputs are finite; a program needn't handle non-finite values.
Results may differ from the reference program's by a relative error of at most 0.0051.
Values may be sent and summed in bfloat16 or wider, within the bound.
A program may use at most 64 MiB of HBM per device.

```python
import jax
import jax.numpy as jnp
from jax import lax

D = 8192
FRAG = 64
WORKERS = 8
TOKENS = 4096


def spiked(result, rng, source, target, shards_of, factor):
    owner, partner = [(jnp.arange(result.shape[axis_at]) // (result.shape[axis_at] // shards_of)).reshape([-1 if axis == axis_at else 1 for axis in range(result.ndim)]) for axis_at in (source, target)]
    chosen = jax.random.permutation(rng, shards_of)[partner]
    strong = (owner == chosen) | (owner == (partner + shards_of // 2) % shards_of)
    return jnp.where(strong, factor * result, result)


def shard_levels(key, extent, cuts, least, high):
    gain = 1.0
    for position, blocks in cuts:
        steps = jax.random.uniform(jax.random.fold_in(jax.random.fold_in(key, 6), position), (blocks,), jnp.float32, least / len(cuts), high / len(cuts))
        gain = gain * jnp.repeat(jnp.exp(steps), extent[position] // blocks).reshape((-1,) + (1,) * (len(extent) - 1 - position))
    return gain


def bell_draw(stream_key, shape, scale, reach, split=(), dtype=jnp.bfloat16):
    values = scale * jax.random.normal(stream_key, shape, jnp.float32)
    if split:
        values = values * shard_levels(stream_key, shape, split, -0.22, 0.18)
    return jnp.clip(values, -reach, reach).astype(dtype)


def bell_draw_with(stream_key, dims, deviation, limit, split, heavy, kind=jnp.bfloat16):
    array = deviation * jax.random.normal(stream_key, dims, jnp.float32)
    if split:
        array = array * shard_levels(stream_key, dims, split, -0.22, 0.18)
    return jnp.clip(spiked(array, jax.random.fold_in(stream_key, 3), *heavy), -limit, limit).astype(kind)


def setup_inputs(seed: int = 0) -> dict:
    splits = jax.random.split(jax.random.key(seed), 5)
    local_weight = bell_draw_with(splits[0], (WORKERS, FRAG, D), FRAG ** -0.5, 1.0, ((0, 8), (2, 4)), (0, 1, 8, 2.0))
    anchor = bell_draw(splits[1], (FRAG, D), FRAG ** -0.5, 0.75, ((1, 4),), jnp.float32)
    momentum = bell_draw(splits[2], (FRAG, D), 0.05, 0.3, ((0, 8), (1, 4)), jnp.float32)
    tokens = bell_draw(splits[3], (TOKENS, FRAG), 1.0, 6.0, ((0, 32),))
    return dict(local_weight=local_weight, anchor=anchor, momentum=momentum, tokens=tokens)


outer_rate = 0.7
decay_rate = 0.9
blend_rate = 0.5


def reference(local_weight, anchor, momentum, tokens):
    pseudo = (anchor[None] - local_weight.astype(jnp.float32)).astype(jnp.bfloat16)
    pseudo = lax.optimization_barrier(pseudo)
    average = jnp.sum(pseudo.astype(jnp.float32), axis=0) / WORKERS
    momentum_out = decay_rate * momentum + average
    anchor_out = anchor - outer_rate * (average + decay_rate * momentum_out)
    blended = (blend_rate * anchor_out[None] + (1.0 - blend_rate) * local_weight.astype(jnp.float32)).astype(jnp.bfloat16)
    grouped = tokens.reshape(WORKERS, TOKENS // WORKERS, FRAG)

    def worker_product(pair):
        rows, weight = pair
        return jnp.dot(rows, weight, preferred_element_type=jnp.float32).astype(jnp.bfloat16)

    product_out = lax.map(worker_product, (grouped, blended)).reshape(TOKENS, D)
    return blended, anchor_out, momentum_out, product_out
```

```python
import functools

import jax
import jax.numpy as jnp
from jax import lax
from jax.experimental import pallas as pl
from jax.experimental.pallas import tpu as pltpu
from jax.sharding import PartitionSpec as P

outer_rate = 0.7
decay_rate = 0.9
blend_rate = 0.5
MESH = pl.DeviceIdType.MESH


def kernel(
    n_r, n_f, chunks, fold,
    lw_ref, anchor_ref, mom_ref, tok_ref,
    blend_ref, aout_ref, mout_ref, prod_ref,
    rs_send, rs_recv, gath,
    rs_ssem, rs_rsem, ag_ssem, ag_rsem, z_ssem, z_rsem,
):
    r = lax.axis_index("replica")
    f = lax.axis_index("fsdp")
    frag, cols = anchor_ref.shape
    rows = frag // n_r
    w = cols // chunks
    half = w // fold

    barrier = pltpu.get_barrier_semaphore()

    def greet(i, _):
        pl.semaphore_signal(
            barrier, inc=1, device_id=(lax.rem(r + i, n_r), f), device_id_type=MESH
        )
        return 0

    lax.fori_loop(1, n_r, greet, 0)

    @pl.when(f > 0)
    def _():
        pl.semaphore_signal(barrier, inc=1, device_id=(r, f - 1), device_id_type=MESH)

    @pl.when(f < n_f - 1)
    def _():
        pl.semaphore_signal(barrier, inc=1, device_id=(r, f + 1), device_id_type=MESH)

    for c in range(chunks):
        for j in range(n_r):
            part = (
                anchor_ref[j * rows : (j + 1) * rows, c * w : (c + 1) * w]
                - lw_ref[0, j * rows : (j + 1) * rows, c * w : (c + 1) * w].astype(jnp.float32)
            )
            part = jnp.concatenate(
                [part[:, k * half : (k + 1) * half] for k in range(fold)], axis=0
            )
            rs_send[c, j] = part.astype(jnp.bfloat16)

    left = (f + n_f - 1) // n_f
    right = (2 * n_f - 2 - f) // n_f
    pl.semaphore_wait(barrier, n_r - 1 + left + right)

    def rs_copy(c, peer, slot):
        return pltpu.make_async_remote_copy(
            src_ref=rs_send.at[c, peer],
            dst_ref=rs_recv.at[c, slot],
            send_sem=rs_ssem.at[c, peer],
            recv_sem=rs_rsem.at[c, slot],
            device_id=(peer, f),
            device_id_type=MESH,
        )

    def ag_copy(c, peer, owner):
        block = aout_ref.at[
            pl.ds(pl.multiple_of(owner * rows, rows), rows), pl.ds(c * w, w)
        ]
        return pltpu.make_async_remote_copy(
            src_ref=block,
            dst_ref=block,
            send_sem=ag_ssem.at[c, peer],
            recv_sem=ag_rsem.at[c, owner],
            device_id=(peer, f),
            device_id_type=MESH,
        )

    def z_copy(c, block, side):
        return pltpu.make_async_remote_copy(
            src_ref=gath.at[block, c],
            dst_ref=gath.at[block, c],
            send_sem=z_ssem.at[c, block, side],
            recv_sem=z_rsem.at[c, block],
            device_id=(r, f + 1 if side == 0 else f - 1),
            device_id_type=MESH,
        )

    def each_peer(body):
        def step(i, _):
            body(lax.rem(r + i, n_r))
            return 0

        lax.fori_loop(1, n_r, step, 0)

    for c in range(chunks):
        each_peer(lambda peer: rs_copy(c, peer, r).start())

    own = pl.ds(pl.multiple_of(r * rows, rows), rows)
    for c in range(chunks):
        at = slice(c * w, (c + 1) * w)

        def arrived(i, total):
            peer = lax.rem(r + i, n_r)
            rs_copy(c, peer, peer).wait_recv()
            return total + rs_recv[c, peer].astype(jnp.float32)

        total = lax.fori_loop(1, n_r, arrived, rs_send[c, r].astype(jnp.float32))
        total = jnp.concatenate(
            [total[k * rows : (k + 1) * rows] for k in range(fold)], axis=1
        )
        average = total / n_r
        mom = decay_rate * mom_ref[:, at] + average
        mout_ref[:, at] = mom
        aout_ref[own, at] = anchor_ref[own, at] - outer_rate * (average + decay_rate * mom)
        each_peer(lambda peer: ag_copy(c, peer, r).start())

    def multiply(c, block):
        prod_ref[:, pl.ds(pl.multiple_of(block * cols + c * w, w), w)] = jnp.dot(
            tok_ref[...], gath[block, c], preferred_element_type=jnp.float32
        ).astype(jnp.bfloat16)

    for c in range(chunks):
        at = slice(c * w, (c + 1) * w)
        each_peer(lambda peer: ag_copy(c, peer, peer).wait_recv())
        blended = (
            blend_rate * aout_ref[:, at]
            + (1.0 - blend_rate) * lw_ref[0, :, at].astype(jnp.float32)
        ).astype(jnp.bfloat16)
        gath[f, c] = blended

        @pl.when(f < n_f - 1)
        def _():
            z_copy(c, f, 0).start()

        @pl.when(f > 0)
        def _():
            z_copy(c, f, 1).start()

        blend_ref[0, :, at] = blended
        multiply(c, f)

    for k in range(1, n_f):
        for c in range(chunks):

            @pl.when(f - k >= 0)
            def _():
                z_copy(c, f - k, 0).wait_recv()

                @pl.when(f < n_f - 1)
                def _():
                    z_copy(c, f - k, 0).start()

            @pl.when(f + k < n_f)
            def _():
                z_copy(c, f + k, 1).wait_recv()

                @pl.when(f > 0)
                def _():
                    z_copy(c, f + k, 1).start()

            @pl.when(f - k >= 0)
            def _():
                multiply(c, f - k)

            @pl.when(f + k < n_f)
            def _():
                multiply(c, f + k)

    for c in range(chunks):

        def sent(peer):
            rs_copy(c, peer, r).wait_send()
            ag_copy(c, peer, r).wait_send()

        each_peer(sent)
        for k in range(n_f):

            @pl.when((f - k >= 0) & (f < n_f - 1))
            def _():
                z_copy(c, f - k, 0).wait_send()

            @pl.when((f + k < n_f) & (f > 0))
            def _():
                z_copy(c, f + k, 1).wait_send()


def per_device(local_weight, anchor, momentum, tokens):
    n_r, n_f = lax.axis_size("replica"), lax.axis_size("fsdp")
    frag, cols = anchor.shape
    rows = frag // n_r
    fold = 1 if rows % 16 == 0 else 2
    chunks = max(1, min(4, cols // (128 * fold)))
    w = cols // chunks
    count = tokens.shape[0]
    vmem = pl.BlockSpec(memory_space=pltpu.VMEM)
    return pl.pallas_call(
        functools.partial(kernel, n_r, n_f, chunks, fold),
        out_shape=(
            jax.ShapeDtypeStruct(local_weight.shape, jnp.bfloat16),
            jax.ShapeDtypeStruct(anchor.shape, jnp.float32),
            jax.ShapeDtypeStruct(momentum.shape, jnp.float32),
            jax.ShapeDtypeStruct((count, cols * n_f), jnp.bfloat16),
        ),
        in_specs=[vmem] * 4,
        out_specs=[vmem] * 4,
        scratch_shapes=[
            pltpu.VMEM((chunks, n_r, rows * fold, w // fold), jnp.bfloat16),
            pltpu.VMEM((chunks, n_r, rows * fold, w // fold), jnp.bfloat16),
            pltpu.VMEM((n_f, chunks, frag, w), jnp.bfloat16),
            pltpu.SemaphoreType.DMA((chunks, n_r)),
            pltpu.SemaphoreType.DMA((chunks, n_r)),
            pltpu.SemaphoreType.DMA((chunks, n_r)),
            pltpu.SemaphoreType.DMA((chunks, n_r)),
            pltpu.SemaphoreType.DMA((chunks, n_f, 2)),
            pltpu.SemaphoreType.DMA((chunks, n_f)),
        ],
        compiler_params=pltpu.CompilerParams(
            collective_id=0, has_side_effects=True, vmem_limit_bytes=40 * 2**20
        ),
        cost_estimate=pl.CostEstimate(
            flops=2 * count * frag * cols * n_f,
            bytes_accessed=4 * frag * cols * 3 + 2 * count * cols * n_f,
            transcendentals=0,
        ),
    )(local_weight, anchor, momentum, tokens)


def solution(mesh):
    placed = (
        P("replica", None, "fsdp"),
        P(None, "fsdp"),
        P("replica", "fsdp"),
        P(("replica", "fsdp"), None),
    )
    return jax.shard_map(
        per_device,
        mesh=mesh,
        in_specs=placed,
        out_specs=placed,
        check_vma=False,
    )
```

```python
import functools

import jax
import jax.numpy as jnp
from jax import lax
from jax.experimental import pallas as pl
from jax.experimental.pallas import tpu as pltpu
from jax.sharding import PartitionSpec as P

outer_rate = 0.7
decay_rate = 0.9
blend_rate = 0.5
MESH = pl.DeviceIdType.MESH


def kernel(
    n_r, n_f, chunks, fold,
    lw_hbm, anchor_hbm, mom_hbm, tok_hbm,
    blend_ref, aout_ref, mout_ref, prod_ref,
    lw_ref, anchor_ref, mom_ref, tok_ref, rs_send, rs_recv, gath, in_sem,
    rs_ssem, rs_rsem, ag_ssem, ag_rsem, z_ssem, z_rsem,
):
    r = lax.axis_index("replica")
    f = lax.axis_index("fsdp")
    fetches = [
        pltpu.make_async_copy(source, target, in_sem.at[i])
        for i, (source, target) in enumerate((
            (lw_hbm, lw_ref), (anchor_hbm, anchor_ref),
            (mom_hbm, mom_ref), (tok_hbm, tok_ref),
        ))
    ]
    for fetch in fetches:
        fetch.start()
    frag, cols = anchor_ref.shape
    rows = frag // n_r
    w = cols // chunks
    half = w // fold

    barrier = pltpu.get_barrier_semaphore()

    def greet(i, _):
        pl.semaphore_signal(
            barrier, inc=1, device_id=(lax.rem(r + i, n_r), f), device_id_type=MESH
        )
        return 0

    lax.fori_loop(1, n_r, greet, 0)

    @pl.when(f > 0)
    def _():
        pl.semaphore_signal(barrier, inc=1, device_id=(r, f - 1), device_id_type=MESH)

    @pl.when(f < n_f - 1)
    def _():
        pl.semaphore_signal(barrier, inc=1, device_id=(r, f + 1), device_id_type=MESH)

    fetches[0].wait()
    fetches[1].wait()

    for c in range(chunks):
        for j in range(n_r):
            part = (
                anchor_ref[j * rows : (j + 1) * rows, c * w : (c + 1) * w]
                - lw_ref[0, j * rows : (j + 1) * rows, c * w : (c + 1) * w].astype(jnp.float32)
            )
            part = jnp.concatenate(
                [part[:, k * half : (k + 1) * half] for k in range(fold)], axis=0
            )
            rs_send[c, j] = part.astype(jnp.bfloat16)

    left = (f + n_f - 1) // n_f
    right = (2 * n_f - 2 - f) // n_f
    pl.semaphore_wait(barrier, n_r - 1 + left + right)

    def rs_copy(c, peer, slot):
        return pltpu.make_async_remote_copy(
            src_ref=rs_send.at[c, peer],
            dst_ref=rs_recv.at[c, slot],
            send_sem=rs_ssem.at[c, peer],
            recv_sem=rs_rsem.at[c, slot],
            device_id=(peer, f),
            device_id_type=MESH,
        )

    def ag_copy(c, peer, owner):
        block = aout_ref.at[
            pl.ds(pl.multiple_of(owner * rows, rows), rows), pl.ds(c * w, w)
        ]
        return pltpu.make_async_remote_copy(
            src_ref=block,
            dst_ref=block,
            send_sem=ag_ssem.at[c, peer],
            recv_sem=ag_rsem.at[c, owner],
            device_id=(peer, f),
            device_id_type=MESH,
        )

    def z_copy(c, block, side):
        return pltpu.make_async_remote_copy(
            src_ref=gath.at[block, c],
            dst_ref=gath.at[block, c],
            send_sem=z_ssem.at[c, block, side],
            recv_sem=z_rsem.at[c, block],
            device_id=(r, f + 1 if side == 0 else f - 1),
            device_id_type=MESH,
        )

    def each_peer(body):
        def step(i, _):
            body(lax.rem(r + i, n_r))
            return 0

        lax.fori_loop(1, n_r, step, 0)

    for c in range(chunks):
        each_peer(lambda peer: rs_copy(c, peer, r).start())

    fetches[2].wait()
    fetches[3].wait()
    own = pl.ds(pl.multiple_of(r * rows, rows), rows)
    for c in range(chunks):
        at = slice(c * w, (c + 1) * w)

        def arrived(i, total):
            peer = lax.rem(r + i, n_r)
            rs_copy(c, peer, peer).wait_recv()
            return total + rs_recv[c, peer].astype(jnp.float32)

        total = lax.fori_loop(1, n_r, arrived, rs_send[c, r].astype(jnp.float32))
        total = jnp.concatenate(
            [total[k * rows : (k + 1) * rows] for k in range(fold)], axis=1
        )
        average = total / n_r
        mom = decay_rate * mom_ref[:, at] + average
        mout_ref[:, at] = mom
        aout_ref[own, at] = anchor_ref[own, at] - outer_rate * (average + decay_rate * mom)
        each_peer(lambda peer: ag_copy(c, peer, r).start())

    def multiply(c, block):
        prod_ref[:, pl.ds(pl.multiple_of(block * cols + c * w, w), w)] = lax.dot_general(
            tok_ref[...],
            gath[block, c],
            (((0,), (0,)), ((), ())),
            preferred_element_type=jnp.float32,
        ).astype(jnp.bfloat16)

    for c in range(chunks):
        at = slice(c * w, (c + 1) * w)
        each_peer(lambda peer: ag_copy(c, peer, peer).wait_recv())
        blended = (
            blend_rate * aout_ref[:, at]
            + (1.0 - blend_rate) * lw_ref[0, :, at].astype(jnp.float32)
        ).astype(jnp.bfloat16)
        gath[f, c] = blended

        @pl.when(f < n_f - 1)
        def _():
            z_copy(c, f, 0).start()

        @pl.when(f > 0)
        def _():
            z_copy(c, f, 1).start()

        blend_ref[0, :, at] = blended
        multiply(c, f)

    for k in range(1, n_f):
        for c in range(chunks):

            @pl.when(f - k >= 0)
            def _():
                z_copy(c, f - k, 0).wait_recv()

                @pl.when(f < n_f - 1)
                def _():
                    z_copy(c, f - k, 0).start()

            @pl.when(f + k < n_f)
            def _():
                z_copy(c, f + k, 1).wait_recv()

                @pl.when(f > 0)
                def _():
                    z_copy(c, f + k, 1).start()

            @pl.when(f - k >= 0)
            def _():
                multiply(c, f - k)

            @pl.when(f + k < n_f)
            def _():
                multiply(c, f + k)

    for c in range(chunks):

        def sent(peer):
            rs_copy(c, peer, r).wait_send()
            ag_copy(c, peer, r).wait_send()

        each_peer(sent)
        for k in range(n_f):

            @pl.when((f - k >= 0) & (f < n_f - 1))
            def _():
                z_copy(c, f - k, 0).wait_send()

            @pl.when((f + k < n_f) & (f > 0))
            def _():
                z_copy(c, f + k, 1).wait_send()


def write_out(*refs):
    count = (len(refs) - 1) // 2
    copies = [
        pltpu.make_async_copy(refs[i], refs[count + i], refs[-1].at[i])
        for i in range(count)
    ]
    for copy in copies:
        copy.start()
    for copy in copies:
        copy.wait()


def per_device(local_weight, anchor, momentum, tokens):
    n_r, n_f = lax.axis_size("replica"), lax.axis_size("fsdp")
    frag, cols = anchor.shape
    rows = frag // n_r
    fold = 1 if rows % 16 == 0 else 2
    chunks = max(1, min(4, cols // (128 * fold)))
    w = cols // chunks
    count = tokens.shape[0]
    hbm = pl.BlockSpec(memory_space=pltpu.HBM)
    vmem = pl.BlockSpec(memory_space=pltpu.VMEM)
    results = pl.pallas_call(
        functools.partial(kernel, n_r, n_f, chunks, fold),
        out_shape=(
            jax.ShapeDtypeStruct(local_weight.shape, jnp.bfloat16),
            jax.ShapeDtypeStruct(anchor.shape, jnp.float32),
            jax.ShapeDtypeStruct(momentum.shape, jnp.float32),
            jax.ShapeDtypeStruct((count, cols * n_f), jnp.bfloat16),
        ),
        in_specs=[hbm] * 4,
        out_specs=[vmem] * 4,
        scratch_shapes=[
            pltpu.VMEM(local_weight.shape, jnp.bfloat16),
            pltpu.VMEM(anchor.shape, jnp.float32),
            pltpu.VMEM(momentum.shape, jnp.float32),
            pltpu.VMEM(tokens.shape[::-1], jnp.bfloat16),
            pltpu.VMEM((chunks, n_r, rows * fold, w // fold), jnp.bfloat16),
            pltpu.VMEM((chunks, n_r, rows * fold, w // fold), jnp.bfloat16),
            pltpu.VMEM((n_f, chunks, frag, w), jnp.bfloat16),
            pltpu.SemaphoreType.DMA((4,)),
            pltpu.SemaphoreType.DMA((chunks, n_r)),
            pltpu.SemaphoreType.DMA((chunks, n_r)),
            pltpu.SemaphoreType.DMA((chunks, n_r)),
            pltpu.SemaphoreType.DMA((chunks, n_r)),
            pltpu.SemaphoreType.DMA((chunks, n_f, 2)),
            pltpu.SemaphoreType.DMA((chunks, n_f)),
        ],
        compiler_params=pltpu.CompilerParams(
            collective_id=0, has_side_effects=True, vmem_limit_bytes=40 * 2**20
        ),
        cost_estimate=pl.CostEstimate(
            flops=2 * count * frag * cols * n_f,
            bytes_accessed=4 * frag * cols * 3 + 2 * count * cols * n_f,
            transcendentals=0,
        ),
    )(*(
        pltpu.with_memory_space_constraint(x, pltpu.HBM)
        for x in (local_weight, anchor, momentum, tokens.T)
    ))
    return pl.pallas_call(
        write_out,
        out_shape=[jax.ShapeDtypeStruct(x.shape, x.dtype) for x in results],
        in_specs=[vmem] * 4,
        out_specs=[hbm] * 4,
        scratch_shapes=[pltpu.SemaphoreType.DMA((4,))],
        compiler_params=pltpu.CompilerParams(vmem_limit_bytes=16 * 2**20),
    )(*results)


def solution(mesh):
    placed = (
        P("replica", None, "fsdp"),
        P(None, "fsdp"),
        P("replica", "fsdp"),
        P(("replica", "fsdp"), None),
    )
    return jax.shard_map(
        per_device,
        mesh=mesh,
        in_specs=placed,
        out_specs=placed,
        check_vma=False,
    )
```

```python
import functools

import jax
import jax.numpy as jnp
from jax import lax
from jax.experimental import pallas as pl
from jax.experimental.pallas import tpu as pltpu
from jax.sharding import PartitionSpec as P

outer_rate = 0.7
decay_rate = 0.9
blend_rate = 0.5
MESH = pl.DeviceIdType.MESH


def kernel(
    n_r, n_f, chunks, fold,
    lw_hbm, anchor_hbm, mom_hbm, tok_hbm,
    blend_ref, aout_ref, mout_ref, prod_ref,
    anchor_ref, mom_ref, tok_ref, rs_send, rs_recv, weights, news, in_sem,
    rs_ssem, rs_rsem, ag_ssem, ag_rsem, z_ssem, z_rsem, n_ssem, n_rsem, d_ssem, d_rsem,
):
    r = lax.axis_index("replica")
    f = lax.axis_index("fsdp")
    frag, cols = anchor_ref.shape
    rows = frag // n_r
    w = cols // chunks
    half = cols // fold

    fetches = [
        pltpu.make_async_copy(source, target, in_sem.at[i])
        for i, (source, target) in enumerate(
            [
                (lw_hbm.at[0, :, pl.ds(c * w, w)], weights.at[f, c])
                for c in range(chunks)
            ]
            + [(anchor_hbm, anchor_ref), (mom_hbm, mom_ref), (tok_hbm, tok_ref)]
        )
    ]
    for fetch in fetches:
        fetch.start()

    barrier = pltpu.get_barrier_semaphore()

    def each_peer(body):
        def step(i, _):
            body(lax.rem(r + i, n_r))
            return 0

        lax.fori_loop(1, n_r, step, 0)

    def each_place(body):
        def step(i, _):
            body(lax.rem(f + i, n_f))
            return 0

        lax.fori_loop(1, n_f, step, 0)

    each_peer(
        lambda peer: pl.semaphore_signal(
            barrier, inc=1, device_id=(peer, f), device_id_type=MESH
        )
    )
    each_place(
        lambda place: pl.semaphore_signal(
            barrier, inc=1, device_id=(r, place), device_id_type=MESH
        )
    )
    for fetch in fetches[: chunks + 1]:
        fetch.wait()

    for j in range(n_r):
        at = slice(j * rows, (j + 1) * rows)
        own_rows = jnp.concatenate(
            [weights[f, c].astype(jnp.float32)[at] for c in range(chunks)], axis=1
        )
        part = anchor_ref[at, :] - own_rows
        rs_send[j] = jnp.concatenate(
            [part[:, k * half : (k + 1) * half] for k in range(fold)], axis=0
        ).astype(jnp.bfloat16)

    pl.semaphore_wait(barrier, n_r + n_f - 2)

    def rs_copy(peer, slot):
        return pltpu.make_async_remote_copy(
            src_ref=rs_send.at[peer],
            dst_ref=rs_recv.at[slot],
            send_sem=rs_ssem.at[peer],
            recv_sem=rs_rsem.at[slot],
            device_id=(peer, f),
            device_id_type=MESH,
        )

    def ag_copy(peer, owner):
        block = aout_ref.at[pl.ds(pl.multiple_of(owner * rows, rows), rows), :]
        return pltpu.make_async_remote_copy(
            src_ref=block,
            dst_ref=block,
            send_sem=ag_ssem.at[peer],
            recv_sem=ag_rsem.at[owner],
            device_id=(peer, f),
            device_id_type=MESH,
        )

    def z_copy(c, block, side):
        return pltpu.make_async_remote_copy(
            src_ref=weights.at[block, c],
            dst_ref=weights.at[block, c],
            send_sem=z_ssem.at[c, block, side],
            recv_sem=z_rsem.at[c, block],
            device_id=(r, f + 1 if side == 0 else f - 1),
            device_id_type=MESH,
        )

    def n_copy(place, block):
        return pltpu.make_async_remote_copy(
            src_ref=news.at[block, r],
            dst_ref=news.at[block, r],
            send_sem=n_ssem.at[place],
            recv_sem=n_rsem.at[block],
            device_id=(r, place),
            device_id_type=MESH,
        )

    def d_copy(peer, block, owner):
        return pltpu.make_async_remote_copy(
            src_ref=news.at[block, owner],
            dst_ref=news.at[block, owner],
            send_sem=d_ssem.at[block, peer],
            recv_sem=d_rsem.at[block, owner],
            device_id=(peer, f),
            device_id_type=MESH,
        )

    def send_on(c, block):
        @pl.when((block <= f) & (f < n_f - 1))
        def _():
            z_copy(c, block, 0).start()

        @pl.when((block >= f) & (f > 0))
        def _():
            z_copy(c, block, 1).start()

    def at_distance(k, body):
        @pl.when(f - k >= 0)
        def _():
            body(f - k)

        @pl.when(f + k < n_f)
        def _():
            body(f + k)

    each_peer(lambda peer: rs_copy(peer, r).start())
    for c in range(chunks):
        send_on(c, f)

    fetches[chunks + 1].wait()
    fetches[chunks + 2].wait()
    own = pl.ds(pl.multiple_of(r * rows, rows), rows)

    each_peer(lambda peer: rs_copy(peer, peer).wait_recv())
    rs_recv[r] = rs_send[r]
    total = rs_recv[0].astype(jnp.float32)
    for j in range(1, n_r):
        total = total + rs_recv[j].astype(jnp.float32)
    total = jnp.concatenate(
        [total[k * rows : (k + 1) * rows] for k in range(fold)], axis=1
    )
    average = total / n_r
    mom = decay_rate * mom_ref[...] + average
    mout_ref[...] = mom
    new = anchor_ref[own, :] - outer_rate * (average + decay_rate * mom)
    aout_ref[own, :] = new
    news[f, r] = jnp.concatenate(
        [new[:, k * half : (k + 1) * half] for k in range(fold)], axis=0
    ).astype(jnp.bfloat16)
    each_place(lambda place: n_copy(place, f).start())
    each_peer(lambda peer: ag_copy(peer, r).start())

    def forward(k):
        for c in range(chunks):

            def body(block):
                z_copy(c, block, 0).wait_recv()
                send_on(c, block)

            at_distance(k, body)

    def spread(k):
        def body(block):
            n_copy(block, block).wait_recv()
            each_peer(lambda peer: d_copy(peer, block, r).start())

        at_distance(k, body)

    def multiply(c, block, weight):
        prod_ref[:, pl.ds(pl.multiple_of(block * cols + c * w, w), w)] = lax.dot_general(
            tok_ref[...],
            weight,
            (((0,), (0,)), ((), ())),
            preferred_element_type=jnp.float32,
        ).astype(jnp.bfloat16)

    def blend(new_rows, weight):
        return (
            blend_rate * new_rows + (1.0 - blend_rate) * weight.astype(jnp.float32)
        ).astype(jnp.bfloat16)

    def finish(k):
        at_distance(
            k,
            lambda block: each_peer(lambda peer: d_copy(peer, block, peer).wait_recv()),
        )
        for c in range(chunks):
            part, start = (c * w) // half, (c * w) % half

            def body(block):
                if k == n_f - 1:
                    z_copy(c, block, 0).wait_recv()
                new_rows = news[block, :, :, start : start + w].astype(jnp.float32)
                new_rows = new_rows[:, part * rows : (part + 1) * rows, :]
                multiply(
                    c, block, blend(new_rows.reshape(frag, w), weights[block, c])
                )

            at_distance(k, body)

    spread(1)
    if n_f > 2:
        forward(1)
    for k in range(2, n_f):
        spread(k)
    each_peer(lambda peer: ag_copy(peer, peer).wait_recv())
    for c in range(chunks):
        at = slice(c * w, (c + 1) * w)
        blended = blend(aout_ref[:, at], weights[f, c])
        blend_ref[0, :, at] = blended
        multiply(c, f, blended)
    for k in range(1, n_f):
        if k + 1 < n_f - 1:
            forward(k + 1)
        finish(k)

    def sent(peer):
        rs_copy(peer, r).wait_send()
        ag_copy(peer, r).wait_send()
        each_place(lambda place: d_copy(peer, place, r).wait_send())

    each_peer(sent)
    each_place(lambda place: n_copy(place, f).wait_send())
    for c in range(chunks):
        for k in range(n_f):

            @pl.when((f - k >= 0) & (f < n_f - 1))
            def _():
                z_copy(c, f - k, 0).wait_send()

            @pl.when((f + k < n_f) & (f > 0))
            def _():
                z_copy(c, f + k, 1).wait_send()


def write_out(*refs):
    count = (len(refs) - 1) // 2
    copies = [
        pltpu.make_async_copy(refs[i], refs[count + i], refs[-1].at[i])
        for i in range(count)
    ]
    for copy in copies:
        copy.start()
    for copy in copies:
        copy.wait()


def per_device(local_weight, anchor, momentum, tokens):
    n_r, n_f = lax.axis_size("replica"), lax.axis_size("fsdp")
    frag, cols = anchor.shape
    rows = frag // n_r
    fold = 1 if rows % 16 == 0 else 2
    chunks = max(1, min(4, cols // (128 * fold)))
    w = cols // chunks
    count = tokens.shape[0]
    hbm = pl.BlockSpec(memory_space=pltpu.HBM)
    vmem = pl.BlockSpec(memory_space=pltpu.VMEM)
    results = pl.pallas_call(
        functools.partial(kernel, n_r, n_f, chunks, fold),
        out_shape=(
            jax.ShapeDtypeStruct(local_weight.shape, jnp.bfloat16),
            jax.ShapeDtypeStruct(anchor.shape, jnp.float32),
            jax.ShapeDtypeStruct(momentum.shape, jnp.float32),
            jax.ShapeDtypeStruct((count, cols * n_f), jnp.bfloat16),
        ),
        in_specs=[hbm] * 4,
        out_specs=[vmem] * 4,
        scratch_shapes=[
            pltpu.VMEM(anchor.shape, jnp.float32),
            pltpu.VMEM(momentum.shape, jnp.float32),
            pltpu.VMEM(tokens.shape[::-1], jnp.bfloat16),
            pltpu.VMEM((n_r, rows * fold, cols // fold), jnp.bfloat16),
            pltpu.VMEM((n_r, rows * fold, cols // fold), jnp.bfloat16),
            pltpu.VMEM((n_f, chunks, frag, w), jnp.bfloat16),
            pltpu.VMEM((n_f, n_r, rows * fold, cols // fold), jnp.bfloat16),
            pltpu.SemaphoreType.DMA((chunks + 3,)),
            pltpu.SemaphoreType.DMA((n_r,)),
            pltpu.SemaphoreType.DMA((n_r,)),
            pltpu.SemaphoreType.DMA((n_r,)),
            pltpu.SemaphoreType.DMA((n_r,)),
            pltpu.SemaphoreType.DMA((chunks, n_f, 2)),
            pltpu.SemaphoreType.DMA((chunks, n_f)),
            pltpu.SemaphoreType.DMA((n_f,)),
            pltpu.SemaphoreType.DMA((n_f,)),
            pltpu.SemaphoreType.DMA((n_f, n_r)),
            pltpu.SemaphoreType.DMA((n_f, n_r)),
        ],
        compiler_params=pltpu.CompilerParams(
            collective_id=0, has_side_effects=True, vmem_limit_bytes=40 * 2**20
        ),
        cost_estimate=pl.CostEstimate(
            flops=2 * count * frag * cols * n_f,
            bytes_accessed=4 * frag * cols * 3 + 2 * count * cols * n_f,
            transcendentals=0,
        ),
    )(*(
        pltpu.with_memory_space_constraint(x, pltpu.HBM)
        for x in (local_weight, anchor, momentum, tokens.T)
    ))
    return pl.pallas_call(
        write_out,
        out_shape=[jax.ShapeDtypeStruct(x.shape, x.dtype) for x in results],
        in_specs=[vmem] * 4,
        out_specs=[hbm] * 4,
        scratch_shapes=[pltpu.SemaphoreType.DMA((4,))],
        compiler_params=pltpu.CompilerParams(vmem_limit_bytes=16 * 2**20),
    )(*results)


def solution(mesh):
    placed = (
        P("replica", None, "fsdp"),
        P(None, "fsdp"),
        P("replica", "fsdp"),
        P(("replica", "fsdp"), None),
    )
    return jax.shard_map(
        per_device,
        mesh=mesh,
        in_specs=placed,
        out_specs=placed,
        check_vma=False,
    )
```

```python
import functools

import jax
import jax.numpy as jnp
from jax import lax
from jax.experimental import pallas as pl
from jax.experimental.pallas import tpu as pltpu
from jax.sharding import PartitionSpec as P

outer_rate = 0.7
decay_rate = 0.9
blend_rate = 0.5
MESH = pl.DeviceIdType.MESH


def kernel(
    n_r, n_f, chunks, fold,
    lw_hbm, anchor_hbm, mom_hbm, tok_hbm,
    blend_ref, aout_ref, mout_ref, prod_ref,
    anchor_ref, mom_ref, tok_ref, rs_send, rs_recv, weights, news, in_sem,
    rs_ssem, rs_rsem, ag_ssem, ag_rsem, z_ssem, z_rsem, n_ssem, n_rsem, d_ssem, d_rsem,
):
    r = lax.axis_index("replica")
    f = lax.axis_index("fsdp")
    frag, cols = anchor_ref.shape
    rows = frag // n_r
    w = cols // chunks
    half = cols // fold

    fetches = [
        pltpu.make_async_copy(source, target, in_sem.at[i])
        for i, (source, target) in enumerate(
            [
                (lw_hbm.at[0, :, pl.ds(c * w, w)], weights.at[f, c])
                for c in range(chunks)
            ]
            + [(anchor_hbm, anchor_ref), (mom_hbm, mom_ref), (tok_hbm, tok_ref)]
        )
    ]
    for fetch in fetches:
        fetch.start()

    barrier = pltpu.get_barrier_semaphore()

    def each_peer(body):
        def step(i, _):
            body(lax.rem(r + i, n_r))
            return 0

        lax.fori_loop(1, n_r, step, 0)

    def mate_of(device):
        return device + 1 - 2 * lax.rem(device, 2)

    mate = mate_of(r)

    def each_far(body):
        def step(i, _):
            body(lax.rem(r + 2 * i, n_r))
            return 0

        lax.fori_loop(1, n_r // 2, step, 0)

    def each_place(body):
        def step(i, _):
            body(lax.rem(f + i, n_f))
            return 0

        lax.fori_loop(1, n_f, step, 0)

    each_peer(
        lambda peer: pl.semaphore_signal(
            barrier, inc=1, device_id=(peer, f), device_id_type=MESH
        )
    )
    each_place(
        lambda place: pl.semaphore_signal(
            barrier, inc=1, device_id=(r, place), device_id_type=MESH
        )
    )
    for fetch in fetches[: chunks + 1]:
        fetch.wait()

    for j in range(n_r):
        at = slice(j * rows, (j + 1) * rows)
        own_rows = jnp.concatenate(
            [weights[f, c].astype(jnp.float32)[at] for c in range(chunks)], axis=1
        )
        part = anchor_ref[at, :] - own_rows
        rs_send[j] = jnp.concatenate(
            [part[:, k * half : (k + 1) * half] for k in range(fold)], axis=0
        ).astype(jnp.bfloat16)

    pl.semaphore_wait(barrier, n_r + n_f - 2)

    def rs_copy(peer, slot):
        return pltpu.make_async_remote_copy(
            src_ref=rs_send.at[peer],
            dst_ref=rs_recv.at[slot],
            send_sem=rs_ssem.at[peer],
            recv_sem=rs_rsem.at[slot],
            device_id=(peer, f),
            device_id_type=MESH,
        )

    def ag_copy(peer, owner, slot):
        block = aout_ref.at[pl.ds(pl.multiple_of(owner * rows, rows), rows), :]
        return pltpu.make_async_remote_copy(
            src_ref=block,
            dst_ref=block,
            send_sem=ag_ssem.at[slot],
            recv_sem=ag_rsem.at[owner],
            device_id=(peer, f),
            device_id_type=MESH,
        )

    def z_copy(c, block, side):
        return pltpu.make_async_remote_copy(
            src_ref=weights.at[block, c],
            dst_ref=weights.at[block, c],
            send_sem=z_ssem.at[c, block, side],
            recv_sem=z_rsem.at[c, block],
            device_id=(r, f + 1 if side == 0 else f - 1),
            device_id_type=MESH,
        )

    def n_copy(place, block):
        return pltpu.make_async_remote_copy(
            src_ref=news.at[block, r],
            dst_ref=news.at[block, r],
            send_sem=n_ssem.at[place],
            recv_sem=n_rsem.at[block],
            device_id=(r, place),
            device_id_type=MESH,
        )

    def d_copy(peer, block, owner, slot):
        return pltpu.make_async_remote_copy(
            src_ref=news.at[block, owner],
            dst_ref=news.at[block, owner],
            send_sem=d_ssem.at[block, slot],
            recv_sem=d_rsem.at[block, owner],
            device_id=(peer, f),
            device_id_type=MESH,
        )

    def send_rows(copy):
        each_far(lambda far: copy(far, r, far).start())
        copy(mate, r, mate).start()

    def relay_rows(copy):
        def step(far):
            copy(far, far, far).wait_recv()
            copy(mate, far, mate_of(far)).start()

        each_far(step)

    def await_rows(copy):
        copy(mate, mate, mate).wait_recv()
        each_far(lambda far: copy(mate, mate_of(far), mate).wait_recv())

    def rows_sent(copy):
        copy(mate, r, mate).wait_send()

        def step(far):
            copy(far, r, far).wait_send()
            copy(mate, far, mate_of(far)).wait_send()

        each_far(step)

    def rows_of(block):
        return lambda peer, owner, slot: d_copy(peer, block, owner, slot)

    def send_on(c, block):
        @pl.when((block <= f) & (f < n_f - 1))
        def _():
            z_copy(c, block, 0).start()

        @pl.when((block >= f) & (f > 0))
        def _():
            z_copy(c, block, 1).start()

    def at_distance(k, body):
        @pl.when(f - k >= 0)
        def _():
            body(f - k)

        @pl.when(f + k < n_f)
        def _():
            body(f + k)

    each_peer(lambda peer: rs_copy(peer, r).start())
    for c in range(chunks):
        send_on(c, f)

    fetches[chunks + 1].wait()
    fetches[chunks + 2].wait()
    own = pl.ds(pl.multiple_of(r * rows, rows), rows)

    each_peer(lambda peer: rs_copy(peer, peer).wait_recv())
    rs_recv[r] = rs_send[r]
    total = rs_recv[0].astype(jnp.float32)
    for j in range(1, n_r):
        total = total + rs_recv[j].astype(jnp.float32)
    total = jnp.concatenate(
        [total[k * rows : (k + 1) * rows] for k in range(fold)], axis=1
    )
    average = total / n_r
    mom = decay_rate * mom_ref[...] + average
    mout_ref[...] = mom
    new = anchor_ref[own, :] - outer_rate * (average + decay_rate * mom)
    aout_ref[own, :] = new
    news[f, r] = jnp.concatenate(
        [new[:, k * half : (k + 1) * half] for k in range(fold)], axis=0
    ).astype(jnp.bfloat16)
    each_place(lambda place: n_copy(place, f).start())
    send_rows(ag_copy)

    def forward(k):
        for c in range(chunks):

            def body(block):
                z_copy(c, block, 0).wait_recv()
                send_on(c, block)

            at_distance(k, body)

    def spread(k):
        def body(block):
            n_copy(block, block).wait_recv()
            send_rows(rows_of(block))

        at_distance(k, body)

    def relay(k):
        at_distance(k, lambda block: relay_rows(rows_of(block)))

    def multiply(c, block, weight):
        prod_ref[:, pl.ds(pl.multiple_of(block * cols + c * w, w), w)] = lax.dot_general(
            tok_ref[...],
            weight,
            (((0,), (0,)), ((), ())),
            preferred_element_type=jnp.float32,
        ).astype(jnp.bfloat16)

    def blend(new_rows, weight):
        return (
            blend_rate * new_rows + (1.0 - blend_rate) * weight.astype(jnp.float32)
        ).astype(jnp.bfloat16)

    def finish(k):
        at_distance(k, lambda block: await_rows(rows_of(block)))
        for c in range(chunks):
            part, start = (c * w) // half, (c * w) % half

            def body(block):
                if k == n_f - 1:
                    z_copy(c, block, 0).wait_recv()
                new_rows = news[block, :, :, start : start + w].astype(jnp.float32)
                new_rows = new_rows[:, part * rows : (part + 1) * rows, :]
                multiply(
                    c, block, blend(new_rows.reshape(frag, w), weights[block, c])
                )

            at_distance(k, body)

    if n_f > 2:
        forward(1)
    spread(1)
    relay_rows(ag_copy)
    for k in range(2, n_f):
        spread(k)
        relay(k - 1)
    await_rows(ag_copy)
    for c in range(chunks):
        at = slice(c * w, (c + 1) * w)
        blended = blend(aout_ref[:, at], weights[f, c])
        blend_ref[0, :, at] = blended
        multiply(c, f, blended)
    for k in range(1, n_f):
        if k + 1 < n_f - 1:
            forward(k + 1)
        if k == 1:
            relay(n_f - 1)
        finish(k)

    each_peer(lambda peer: rs_copy(peer, r).wait_send())
    rows_sent(ag_copy)
    each_place(lambda place: rows_sent(rows_of(place)))
    each_place(lambda place: n_copy(place, f).wait_send())
    for c in range(chunks):
        for k in range(n_f):

            @pl.when((f - k >= 0) & (f < n_f - 1))
            def _():
                z_copy(c, f - k, 0).wait_send()

            @pl.when((f + k < n_f) & (f > 0))
            def _():
                z_copy(c, f + k, 1).wait_send()


def write_out(*refs):
    count = (len(refs) - 1) // 2
    copies = [
        pltpu.make_async_copy(refs[i], refs[count + i], refs[-1].at[i])
        for i in range(count)
    ]
    for copy in copies:
        copy.start()
    for copy in copies:
        copy.wait()


def per_device(local_weight, anchor, momentum, tokens):
    n_r, n_f = lax.axis_size("replica"), lax.axis_size("fsdp")
    frag, cols = anchor.shape
    rows = frag // n_r
    fold = 1 if rows % 16 == 0 else 2
    chunks = max(1, min(4, cols // (128 * fold)))
    w = cols // chunks
    count = tokens.shape[0]
    hbm = pl.BlockSpec(memory_space=pltpu.HBM)
    vmem = pl.BlockSpec(memory_space=pltpu.VMEM)
    results = pl.pallas_call(
        functools.partial(kernel, n_r, n_f, chunks, fold),
        out_shape=(
            jax.ShapeDtypeStruct(local_weight.shape, jnp.bfloat16),
            jax.ShapeDtypeStruct(anchor.shape, jnp.float32),
            jax.ShapeDtypeStruct(momentum.shape, jnp.float32),
            jax.ShapeDtypeStruct((count, cols * n_f), jnp.bfloat16),
        ),
        in_specs=[hbm] * 4,
        out_specs=[vmem] * 4,
        scratch_shapes=[
            pltpu.VMEM(anchor.shape, jnp.float32),
            pltpu.VMEM(momentum.shape, jnp.float32),
            pltpu.VMEM(tokens.shape[::-1], jnp.bfloat16),
            pltpu.VMEM((n_r, rows * fold, cols // fold), jnp.bfloat16),
            pltpu.VMEM((n_r, rows * fold, cols // fold), jnp.bfloat16),
            pltpu.VMEM((n_f, chunks, frag, w), jnp.bfloat16),
            pltpu.VMEM((n_f, n_r, rows * fold, cols // fold), jnp.bfloat16),
            pltpu.SemaphoreType.DMA((chunks + 3,)),
            pltpu.SemaphoreType.DMA((n_r,)),
            pltpu.SemaphoreType.DMA((n_r,)),
            pltpu.SemaphoreType.DMA((n_r,)),
            pltpu.SemaphoreType.DMA((n_r,)),
            pltpu.SemaphoreType.DMA((chunks, n_f, 2)),
            pltpu.SemaphoreType.DMA((chunks, n_f)),
            pltpu.SemaphoreType.DMA((n_f,)),
            pltpu.SemaphoreType.DMA((n_f,)),
            pltpu.SemaphoreType.DMA((n_f, n_r)),
            pltpu.SemaphoreType.DMA((n_f, n_r)),
        ],
        compiler_params=pltpu.CompilerParams(
            collective_id=0, has_side_effects=True, vmem_limit_bytes=40 * 2**20
        ),
        cost_estimate=pl.CostEstimate(
            flops=2 * count * frag * cols * n_f,
            bytes_accessed=4 * frag * cols * 3 + 2 * count * cols * n_f,
            transcendentals=0,
        ),
    )(*(
        pltpu.with_memory_space_constraint(x, pltpu.HBM)
        for x in (local_weight, anchor, momentum, tokens.T)
    ))
    return pl.pallas_call(
        write_out,
        out_shape=[jax.ShapeDtypeStruct(x.shape, x.dtype) for x in results],
        in_specs=[vmem] * 4,
        out_specs=[hbm] * 4,
        scratch_shapes=[pltpu.SemaphoreType.DMA((4,))],
        compiler_params=pltpu.CompilerParams(vmem_limit_bytes=16 * 2**20),
    )(*results)


def solution(mesh):
    placed = (
        P("replica", None, "fsdp"),
        P(None, "fsdp"),
        P("replica", "fsdp"),
        P(("replica", "fsdp"), None),
    )
    return jax.shard_map(
        per_device,
        mesh=mesh,
        in_specs=placed,
        out_specs=placed,
        check_vma=False,
    )
```

```python
import functools

import jax
import jax.numpy as jnp
from jax import lax
from jax.experimental import pallas as pl
from jax.experimental.pallas import tpu as pltpu
from jax.sharding import PartitionSpec as P

outer_rate = 0.7
decay_rate = 0.9
blend_rate = 0.5
MESH = pl.DeviceIdType.MESH


def kernel(
    n_r, n_f, chunks, fold,
    lw_hbm, anchor_hbm, mom_hbm, tok_hbm,
    blend_ref, aout_ref, mout_ref, prod_ref,
    anchor_ref, mom_ref, tok_ref, rs_send, rs_recv, weights, news, in_sem,
    rs_ssem, rs_rsem, ag_ssem, ag_rsem, z_ssem, z_rsem, n_ssem, n_rsem, d_ssem, d_rsem,
):
    r = lax.axis_index("replica")
    f = lax.axis_index("fsdp")
    frag, cols = anchor_ref.shape
    rows = frag // n_r
    w = cols // chunks
    half = cols // fold

    fetches = [
        pltpu.make_async_copy(source, target, in_sem.at[i])
        for i, (source, target) in enumerate(
            [
                (lw_hbm.at[0, :, pl.ds(c * w, w)], weights.at[f, c])
                for c in range(chunks)
            ]
            + [(anchor_hbm, anchor_ref), (mom_hbm, mom_ref), (tok_hbm, tok_ref)]
        )
    ]
    for fetch in fetches:
        fetch.start()

    barrier = pltpu.get_barrier_semaphore()

    def each_peer(body):
        def step(i, _):
            body(lax.rem(r + i, n_r))
            return 0

        lax.fori_loop(1, n_r, step, 0)

    def mate_of(device):
        return device + 1 - 2 * lax.rem(device, 2)

    mate = mate_of(r)

    def each_far(body):
        def step(i, _):
            body(lax.rem(r + 2 * i, n_r))
            return 0

        lax.fori_loop(1, n_r // 2, step, 0)

    def each_place(body):
        def step(i, _):
            body(lax.rem(f + i, n_f))
            return 0

        lax.fori_loop(1, n_f, step, 0)

    each_peer(
        lambda peer: pl.semaphore_signal(
            barrier, inc=1, device_id=(peer, f), device_id_type=MESH
        )
    )
    each_place(
        lambda place: pl.semaphore_signal(
            barrier, inc=1, device_id=(r, place), device_id_type=MESH
        )
    )
    for fetch in fetches[: chunks + 1]:
        fetch.wait()

    for j in range(n_r):
        at = slice(j * rows, (j + 1) * rows)
        own_rows = jnp.concatenate(
            [weights[f, c].astype(jnp.float32)[at] for c in range(chunks)], axis=1
        )
        part = anchor_ref[at, :] - own_rows
        rs_send[j] = jnp.concatenate(
            [part[:, k * half : (k + 1) * half] for k in range(fold)], axis=0
        ).astype(jnp.bfloat16)

    pl.semaphore_wait(barrier, n_r + n_f - 2)

    def rs_copy(peer, slot):
        return pltpu.make_async_remote_copy(
            src_ref=rs_send.at[peer],
            dst_ref=rs_recv.at[slot],
            send_sem=rs_ssem.at[peer],
            recv_sem=rs_rsem.at[slot],
            device_id=(peer, f),
            device_id_type=MESH,
        )

    def ag_copy(peer, owner, slot):
        block = aout_ref.at[pl.ds(pl.multiple_of(owner * rows, rows), rows), :]
        return pltpu.make_async_remote_copy(
            src_ref=block,
            dst_ref=block,
            send_sem=ag_ssem.at[slot],
            recv_sem=ag_rsem.at[owner],
            device_id=(peer, f),
            device_id_type=MESH,
        )

    def z_copy(c, block, side):
        return pltpu.make_async_remote_copy(
            src_ref=weights.at[block, c],
            dst_ref=weights.at[block, c],
            send_sem=z_ssem.at[c, block, side],
            recv_sem=z_rsem.at[c, block],
            device_id=(r, f + 1 if side == 0 else f - 1),
            device_id_type=MESH,
        )

    def n_copy(place, block):
        return pltpu.make_async_remote_copy(
            src_ref=news.at[block, r],
            dst_ref=news.at[block, r],
            send_sem=n_ssem.at[place],
            recv_sem=n_rsem.at[block],
            device_id=(r, place),
            device_id_type=MESH,
        )

    def d_copy(peer, block, owner, slot):
        return pltpu.make_async_remote_copy(
            src_ref=news.at[block, owner],
            dst_ref=news.at[block, owner],
            send_sem=d_ssem.at[block, slot],
            recv_sem=d_rsem.at[block, owner],
            device_id=(peer, f),
            device_id_type=MESH,
        )

    def send_rows(copy):
        each_far(lambda far: copy(far, r, far).start())
        copy(mate, r, mate).start()

    def relay_rows(copy):
        def step(far):
            copy(far, far, far).wait_recv()
            copy(mate, far, mate_of(far)).start()

        each_far(step)

    def await_rows(copy):
        copy(mate, mate, mate).wait_recv()
        each_far(lambda far: copy(mate, mate_of(far), mate).wait_recv())

    def rows_sent(copy):
        copy(mate, r, mate).wait_send()

        def step(far):
            copy(far, r, far).wait_send()
            copy(mate, far, mate_of(far)).wait_send()

        each_far(step)

    def rows_of(block):
        return lambda peer, owner, slot: d_copy(peer, block, owner, slot)

    def send_on(c, block):
        @pl.when((block <= f) & (f < n_f - 1))
        def _():
            z_copy(c, block, 0).start()

        @pl.when((block >= f) & (f > 0))
        def _():
            z_copy(c, block, 1).start()

    def at_distance(k, body):
        @pl.when(f - k >= 0)
        def _():
            body(f - k)

        @pl.when(f + k < n_f)
        def _():
            body(f + k)

    each_peer(lambda peer: rs_copy(peer, r).start())
    for c in range(chunks):
        send_on(c, f)

    fetches[chunks + 1].wait()
    fetches[chunks + 2].wait()
    own = pl.ds(pl.multiple_of(r * rows, rows), rows)

    each_peer(lambda peer: rs_copy(peer, peer).wait_recv())
    rs_recv[r] = rs_send[r]
    total = rs_recv[0].astype(jnp.float32)
    for j in range(1, n_r):
        total = total + rs_recv[j].astype(jnp.float32)
    total = jnp.concatenate(
        [total[k * rows : (k + 1) * rows] for k in range(fold)], axis=1
    )
    average = total / n_r
    mom = decay_rate * mom_ref[...] + average
    mout_ref[...] = mom
    new = anchor_ref[own, :] - outer_rate * (average + decay_rate * mom)
    aout_ref[own, :] = new
    news[f, r] = jnp.concatenate(
        [new[:, k * half : (k + 1) * half] for k in range(fold)], axis=0
    ).astype(jnp.bfloat16)
    each_place(lambda place: n_copy(place, f).start())
    send_rows(ag_copy)

    def forward(k):
        for c in range(chunks):

            def body(block):
                z_copy(c, block, 0).wait_recv()
                send_on(c, block)

            at_distance(k, body)

    def spread(k):
        def body(block):
            n_copy(block, block).wait_recv()
            send_rows(rows_of(block))

        at_distance(k, body)

    def relay(k):
        at_distance(k, lambda block: relay_rows(rows_of(block)))

    def multiply(c, block, weight):
        prod_ref[:, pl.ds(pl.multiple_of(block * cols + c * w, w), w)] = lax.dot_general(
            tok_ref[...],
            weight,
            (((0,), (0,)), ((), ())),
            preferred_element_type=jnp.float32,
        ).astype(jnp.bfloat16)

    def blend(new_rows, weight):
        return (
            blend_rate * new_rows + (1.0 - blend_rate) * weight.astype(jnp.float32)
        ).astype(jnp.bfloat16)

    def finish(k):
        at_distance(k, lambda block: await_rows(rows_of(block)))
        for c in range(chunks):
            part, start = (c * w) // half, (c * w) % half

            def body(block):
                if k == n_f - 1:
                    z_copy(c, block, 0).wait_recv()
                new_rows = news[block, :, :, start : start + w].astype(jnp.float32)
                new_rows = new_rows[:, part * rows : (part + 1) * rows, :]
                multiply(
                    c, block, blend(new_rows.reshape(frag, w), weights[block, c])
                )

            at_distance(k, body)

    if n_f > 2:
        forward(1)
    spread(1)
    relay_rows(ag_copy)
    for k in range(2, n_f):
        spread(k)
        relay(k - 1)
    if n_f > 3:
        forward(2)
    await_rows(ag_copy)
    for c in range(chunks):
        at = slice(c * w, (c + 1) * w)
        blended = blend(aout_ref[:, at], weights[f, c])
        blend_ref[0, :, at] = blended
        multiply(c, f, blended)
    for k in range(1, n_f):
        if 1 < k < n_f - 2:
            forward(k + 1)
        if k == 1:
            relay(n_f - 1)
        finish(k)

    each_peer(lambda peer: rs_copy(peer, r).wait_send())
    rows_sent(ag_copy)
    each_place(lambda place: rows_sent(rows_of(place)))
    each_place(lambda place: n_copy(place, f).wait_send())
    for c in range(chunks):
        for k in range(n_f):

            @pl.when((f - k >= 0) & (f < n_f - 1))
            def _():
                z_copy(c, f - k, 0).wait_send()

            @pl.when((f + k < n_f) & (f > 0))
            def _():
                z_copy(c, f + k, 1).wait_send()


def write_out(*refs):
    count = (len(refs) - 1) // 2
    copies = [
        pltpu.make_async_copy(refs[i], refs[count + i], refs[-1].at[i])
        for i in range(count)
    ]
    for copy in copies:
        copy.start()
    for copy in copies:
        copy.wait()


def per_device(local_weight, anchor, momentum, tokens):
    n_r, n_f = lax.axis_size("replica"), lax.axis_size("fsdp")
    frag, cols = anchor.shape
    rows = frag // n_r
    fold = 1 if rows % 16 == 0 else 2
    chunks = max(1, min(4, cols // (128 * fold)))
    w = cols // chunks
    count = tokens.shape[0]
    hbm = pl.BlockSpec(memory_space=pltpu.HBM)
    vmem = pl.BlockSpec(memory_space=pltpu.VMEM)
    results = pl.pallas_call(
        functools.partial(kernel, n_r, n_f, chunks, fold),
        out_shape=(
            jax.ShapeDtypeStruct(local_weight.shape, jnp.bfloat16),
            jax.ShapeDtypeStruct(anchor.shape, jnp.float32),
            jax.ShapeDtypeStruct(momentum.shape, jnp.float32),
            jax.ShapeDtypeStruct((count, cols * n_f), jnp.bfloat16),
        ),
        in_specs=[hbm] * 4,
        out_specs=[vmem] * 4,
        scratch_shapes=[
            pltpu.VMEM(anchor.shape, jnp.float32),
            pltpu.VMEM(momentum.shape, jnp.float32),
            pltpu.VMEM(tokens.shape[::-1], jnp.bfloat16),
            pltpu.VMEM((n_r, rows * fold, cols // fold), jnp.bfloat16),
            pltpu.VMEM((n_r, rows * fold, cols // fold), jnp.bfloat16),
            pltpu.VMEM((n_f, chunks, frag, w), jnp.bfloat16),
            pltpu.VMEM((n_f, n_r, rows * fold, cols // fold), jnp.bfloat16),
            pltpu.SemaphoreType.DMA((chunks + 3,)),
            pltpu.SemaphoreType.DMA((n_r,)),
            pltpu.SemaphoreType.DMA((n_r,)),
            pltpu.SemaphoreType.DMA((n_r,)),
            pltpu.SemaphoreType.DMA((n_r,)),
            pltpu.SemaphoreType.DMA((chunks, n_f, 2)),
            pltpu.SemaphoreType.DMA((chunks, n_f)),
            pltpu.SemaphoreType.DMA((n_f,)),
            pltpu.SemaphoreType.DMA((n_f,)),
            pltpu.SemaphoreType.DMA((n_f, n_r)),
            pltpu.SemaphoreType.DMA((n_f, n_r)),
        ],
        compiler_params=pltpu.CompilerParams(
            collective_id=0, has_side_effects=True, vmem_limit_bytes=40 * 2**20
        ),
        cost_estimate=pl.CostEstimate(
            flops=2 * count * frag * cols * n_f,
            bytes_accessed=4 * frag * cols * 3 + 2 * count * cols * n_f,
            transcendentals=0,
        ),
    )(*(
        pltpu.with_memory_space_constraint(x, pltpu.HBM)
        for x in (local_weight, anchor, momentum, tokens.T)
    ))
    return pl.pallas_call(
        write_out,
        out_shape=[jax.ShapeDtypeStruct(x.shape, x.dtype) for x in results],
        in_specs=[vmem] * 4,
        out_specs=[hbm] * 4,
        scratch_shapes=[pltpu.SemaphoreType.DMA((4,))],
        compiler_params=pltpu.CompilerParams(vmem_limit_bytes=16 * 2**20),
    )(*results)


def solution(mesh):
    placed = (
        P("replica", None, "fsdp"),
        P(None, "fsdp"),
        P("replica", "fsdp"),
        P(("replica", "fsdp"), None),
    )
    return jax.shard_map(
        per_device,
        mesh=mesh,
        in_specs=placed,
        out_specs=placed,
        check_vma=False,
    )
```
